512 devices in a mesh: section: 32 (over z, x), leaf: 16 (over y, core).
Axes of the slice: x: 4, y: 8, z: 8, core: 2. Of those that a mesh axis runs over, the one named last changes fastest.
Arguments:
- query_feats: bfloat16 [65536, 300], P(('section', 'leaf')), may hold values from -6 to 6
- query_weight: float32 [65536], P('section'), may hold values from 0.02 to 0.2
- positive_label: int32 [65536, 8], P('section'), may hold values from 0 to 131071, as said below
- positive_bucket: int32 [65536, 8], P('section'), may hold values from 0 to 15
- inv_prop: float32 [16], replicated, may hold values from 1 to 10
- primary_w: bfloat16 [131072, 300], P(('section', 'leaf')), may hold values from -0.375 to 0.375
- copy_owner: int32 [131072], P(('section', 'leaf')), may hold values from 0 to 31, as said below
- copy_row: int32 [131072], P(('section', 'leaf')), may hold values from 0 to 255
Outputs:
- query_grad: float32 [65536, 300], P(('section', 'leaf'))
- primary_grad: float32 [131072, 300], P(('section', 'leaf'))
The draws below stay inside these ranges and needn't reach their ends.
Inputs may be any that keep to these rules, and one draw needn't show every extreme that they name: `copy_owner`: each copy names a section other than its own device's; among the copies of one device at most 16 name one owner, and exactly 16 name one of them. `positive_label`: every listed label is the label of some slot, primary or copy, of the query's own section; a label may be listed twice.
All inputs are finite; a program needn't handle non-finite values.
Results may differ from the reference program's by a relative error of at most 0.0018.
Values may be sent and summed in bfloat16 or wider, within the bound.
No kernel may reach another device: no remote copies, remote signals or barrier semaphores. Data moves between devices by JAX's collectives and lax.ppermute only.
A program may use at most 64 MiB of HBM per device.

```python
import math
import jax
import jax.numpy as jnp
from jax import lax

D = 300
PRIM_DEV = 256
POS = 8
BUCKETS = 16
COPY_DEV = 256
CAP = 16
Q_SECTION = 2048
Q_TOTAL = 65536
PRIMS = 131072
N_SECTION = 32
N_LEAF = 16


def copy_map(key):
    base_key = jax.random.fold_in(key, 7)
    key_coin, key_peer, key_shuffle, key_rows = jax.random.split(base_key, 4)
    devices = N_SECTION * N_LEAF
    slots = jnp.arange(COPY_DEV, dtype=jnp.int32)
    coin = jax.random.randint(key_coin, (devices, COPY_DEV), 0, 2)
    group = jnp.where(slots[None, :] < CAP, 0, 1 + (slots[None, :] - CAP + coin) % (N_SECTION - 2))
    peer_scores = jax.random.randint(key_peer, (devices, N_SECTION - 1), 0, 1 << 20) * N_SECTION + jnp.arange(N_SECTION - 1, dtype=jnp.int32)[None, :]
    peer_order = jnp.argsort(peer_scores, axis=1).astype(jnp.int32)
    other = jnp.take_along_axis(peer_order, group, axis=1)
    own_section = (jnp.arange(devices, dtype=jnp.int32) // N_LEAF)[:, None]
    owner = (own_section + 1 + other) % N_SECTION
    slot_scores = jax.random.randint(key_shuffle, (devices, COPY_DEV), 0, 1 << 20) * COPY_DEV + slots[None, :]
    shuffle = jnp.argsort(slot_scores, axis=1).astype(jnp.int32)
    owner = jnp.take_along_axis(owner, shuffle, axis=1)
    rows_drawn = jax.random.randint(key_rows, (devices, COPY_DEV), 0, PRIM_DEV)
    return (owner.astype(jnp.int32), rows_drawn.astype(jnp.int32))


def draw_copy_owner(key, part):
    return copy_map(key)[0].reshape(-1).astype(jnp.int32)


def draw_copy_row(key, part):
    return copy_map(key)[1].reshape(-1).astype(jnp.int32)


def draw_positive_label(key, part):
    owner, rows_drawn = copy_map(key)
    pick_key = jax.random.fold_in(key, 11)
    key_leaf, key_slot = jax.random.split(pick_key, 2)
    query_section = (jnp.arange(Q_TOTAL, dtype=jnp.int32) // Q_SECTION)[:, None]
    leaf_pick = jax.random.randint(key_leaf, (Q_TOTAL, POS), 0, N_LEAF)
    slot_pick = jax.random.randint(key_slot, (Q_TOTAL, POS), 0, PRIM_DEV + COPY_DEV)
    device = query_section * N_LEAF + leaf_pick
    prim_label = device * PRIM_DEV + slot_pick
    copy_index = jnp.clip(slot_pick - PRIM_DEV, 0, COPY_DEV - 1)
    copy_owner_of = owner[device, copy_index]
    copy_row_of = rows_drawn[device, copy_index]
    copy_label = (copy_owner_of * N_LEAF + leaf_pick) * PRIM_DEV + copy_row_of
    return jnp.where(slot_pick < PRIM_DEV, prim_label, copy_label).astype(jnp.int32)


def place_ends(array, own_key, low, largest):
    spot = [jax.random.randint(jax.random.fold_in(own_key, axis), (), 0, length) for axis, length in enumerate(array.shape)]
    widest = array.shape.index(max(array.shape))
    beside = spot[:widest] + [(spot[widest] + 1) % array.shape[widest]] + spot[widest + 1:]
    return array.at[tuple(spot)].set(low).at[tuple(beside)].set(largest)


def block_scale(own_key, dims, cuts, least, high):
    def one(dim, parts):
        steps = jax.random.uniform(jax.random.fold_in(jax.random.fold_in(own_key, 6), dim), (parts,), jnp.float32, least / len(cuts), high / len(cuts))
        return jnp.repeat(jnp.exp(steps), dims[dim] // parts).reshape((-1,) + (1,) * (len(dims) - dim - 1))

    gain = one(*cuts[0])
    for cut in cuts[1:]:
        gain = gain * one(*cut)
    return gain


def bell_draw(key, shape, spread, bound, shards=(), kind=jnp.bfloat16):
    loudness = block_scale(key, shape, shards, -0.22, 0.18) if shards else 1.0
    array = jax.random.normal(key, shape, jnp.float32) * spread * loudness
    return jnp.minimum(jnp.maximum(array, -bound), bound).astype(kind)


def setup_inputs(seed: int = 0) -> dict:
    key_of = jax.random.split(jax.random.key(seed), 9)
    return {
        "query_feats": bell_draw(key_of[0], (Q_TOTAL, D), 1.0, 6.0, ((0, 512),)),
        "query_weight": jnp.clip(jnp.exp(math.log(0.2) - 2.3025851 * jax.random.uniform(key_of[1], (Q_TOTAL,), jnp.float32) ** block_scale(key_of[1], (Q_TOTAL,), ((0, 32),), -0.2, 0.2)), 0.02, 0.2),
        "positive_label": draw_positive_label(jax.random.fold_in(key_of[8], 71), 0),
        "positive_bucket": place_ends(jax.random.randint(key_of[3], (Q_TOTAL, POS), 0, BUCKETS), jax.random.fold_in(key_of[3], 1), 0, BUCKETS - 1).astype(jnp.int32),
        "inv_prop": jnp.clip(jnp.exp(jax.random.uniform(key_of[4], (BUCKETS,), jnp.float32, math.log(1.0), math.log(10.0))), 1.0, 10.0),
        "primary_w": bell_draw(key_of[5], (PRIMS, D), D ** -0.5, 0.375, ((0, 512),)),
        "copy_owner": draw_copy_owner(jax.random.fold_in(key_of[8], 71), 0),
        "copy_row": draw_copy_row(jax.random.fold_in(key_of[8], 71), 0),
    }


def coefficients(queries, scales, positives, values, weights, labels):
    logits = jnp.dot(queries, weights.T, preferred_element_type=jnp.float32)
    sigmoid_val = jax.nn.sigmoid(logits)
    hit_count = jnp.zeros(logits.shape, jnp.float32)
    pos_weight = jnp.zeros(logits.shape, jnp.float32)
    for column in range(positives.shape[1]):
        matched = (labels[None, :] == positives[:, column:column + 1]).astype(jnp.float32)
        hit_count = hit_count + matched
        pos_weight = pos_weight + matched * values[:, column:column + 1]
    mixed = (1.0 - jnp.minimum(hit_count, 1.0)) * sigmoid_val + pos_weight * (sigmoid_val - 1.0)
    return (scales[:, None] * mixed).astype(jnp.bfloat16)


def reference(query_feats, query_weight, positive_label, positive_bucket, inv_prop, primary_w, copy_owner, copy_row):
    values_all = inv_prop[positive_bucket].astype(jnp.float32)
    feats = query_feats.reshape(N_SECTION, Q_SECTION, D)
    scales = query_weight.reshape(N_SECTION, Q_SECTION)
    positives = positive_label.reshape(N_SECTION, Q_SECTION, POS)
    values = values_all.reshape(N_SECTION, Q_SECTION, POS)
    grid = primary_w.reshape(N_SECTION, N_LEAF, PRIM_DEV, D)
    owners = copy_owner.reshape(N_SECTION, N_LEAF, COPY_DEV)
    copy_rows = copy_row.reshape(N_SECTION, N_LEAF, COPY_DEV)

    def visit(carry, device):
        query_total, prim_total = carry
        section = device // N_LEAF
        leaf_num = device % N_LEAF
        owner_row = owners[section, leaf_num]
        copy_index = copy_rows[section, leaf_num]
        copy_w = grid[owner_row, leaf_num, copy_index]
        weights = jnp.concatenate([grid[section, leaf_num], copy_w], axis=0)
        prim_ids = (section * N_LEAF + leaf_num) * PRIM_DEV + jnp.arange(PRIM_DEV, dtype=jnp.int32)
        copy_ids = (owner_row * N_LEAF + leaf_num) * PRIM_DEV + copy_index
        labels = jnp.concatenate([prim_ids, copy_ids]).astype(jnp.int32)
        coefficient = coefficients(feats[section], scales[section], positives[section], values[section], weights, labels)
        query_part = jnp.dot(coefficient, weights, preferred_element_type=jnp.float32)
        slot_part = jnp.dot(coefficient.T, feats[section], preferred_element_type=jnp.float32)
        query_total = query_total.at[section].add(query_part)
        prim_total = prim_total.at[labels].add(slot_part)
        return (query_total, prim_total), None

    start_state = (jnp.zeros((N_SECTION, Q_SECTION, D), jnp.float32), jnp.zeros((PRIMS, D), jnp.float32))
    devices = jnp.arange(N_SECTION * N_LEAF, dtype=jnp.int32)
    (query_total, prim_total), _ = lax.scan(visit, start_state, devices)
    return query_total.reshape(Q_TOTAL, D), prim_total
```

```python
import functools

import jax
import jax.numpy as jnp
from jax import lax
from jax.experimental import pallas as pl
from jax.experimental.pallas import tpu as pltpu
from jax.sharding import PartitionSpec as P

BF16 = jnp.bfloat16
F32 = jnp.float32
I32 = jnp.int32
LANES = 128
CAP = 16
ROW_CHUNK = 32

VMEM = pl.BlockSpec(memory_space=pltpu.VMEM)
SMEM = pl.BlockSpec(memory_space=pltpu.SMEM)
PARAMS = pltpu.CompilerParams(vmem_limit_bytes=40 * 2**20)


def iota(shape, dim):
    return lax.broadcasted_iota(I32, shape, dim)


def ones(mask):
    return jnp.where(mask, 1.0, 0.0).astype(BF16)


def nt(a, b):
    return lax.dot_general(a, b, (((1,), (1,)), ((), ())), preferred_element_type=F32)


def nn(a, b):
    return lax.dot_general(a, b, (((1,), (0,)), ((), ())), preferred_element_type=F32)


def tn(a, b):
    return lax.dot_general(a, b, (((0,), (0,)), ((), ())), preferred_element_type=F32)


def call(kernel, out, ins, scratch=(), flops=0, size=0):
    return pl.pallas_call(
        kernel,
        out_shape=out,
        in_specs=ins,
        out_specs=jax.tree.map(lambda _: VMEM, out),
        scratch_shapes=scratch,
        compiler_params=PARAMS,
        cost_estimate=pl.CostEstimate(flops=flops, bytes_accessed=size, transcendentals=0),
    )


def ranks(owner, sections):
    n = owner.shape[1]
    hot = owner == iota((sections, n), 0)
    upper = ones(iota((n, n), 0) < iota((n, n), 1))
    before = nn(ones(hot), upper)
    return hot, jnp.sum(jnp.where(hot, before, 0.0), axis=0, keepdims=True)


def ask_kernel(owner_ref, row_ref, ask_ref):
    sections = ask_ref.shape[0]
    owner = owner_ref[...]
    hot, rank = ranks(owner, sections)
    rows = jnp.where(hot, row_ref[...].astype(F32) + 1.0, 0.0).astype(BF16)
    place = ones(iota((LANES, owner.shape[1]), 0).astype(F32) == rank)
    ask_ref[...] = nt(rows, place).reshape(ask_ref.shape)


def wanted_hot(ask, prim):
    sections = ask.shape[0]
    places = sections * CAP
    spread = ones(iota((places, sections), 0) // CAP == iota((places, sections), 1))
    every = nn(spread, ask.astype(BF16))
    mine = iota((places, LANES), 0) % CAP == iota((places, LANES), 1)
    column = jnp.sum(jnp.where(mine, every, 0.0), axis=1, keepdims=True)
    return ones(iota((places, prim), 1).astype(F32) + 1.0 == column)


def serve_kernel(ask_ref, wt_ref, served_ref):
    ask = ask_ref[...].reshape(ask_ref.shape[0], LANES)
    hot = wanted_hot(ask, wt_ref.shape[1])
    served_ref[...] = nt(hot, wt_ref[...]).astype(BF16).reshape(served_ref.shape)


def prepare_kernel(
    first_ref, prop_ref, owner_ref, row_ref, wt_ref, bucket_ref, weight_ref,
    comp_ref, comp_t_ref, slots_ref, wrow_ref, value_ref,
):
    sections = comp_ref.shape[1] // CAP
    owner = owner_ref[...]
    prim = wt_ref.shape[1]
    n = owner.shape[1]
    _, rank = ranks(owner, sections)
    target = owner.astype(F32) * CAP + rank
    places = sections * CAP
    comp_t_ref[...] = ones(iota((places, n), 0).astype(F32) == target)
    target_col = jnp.broadcast_to(target, (LANES, n)).T
    for block in range(places // LANES):
        comp_ref[:, block * LANES:(block + 1) * LANES] = ones(
            (iota((n, LANES), 1) + block * LANES).astype(F32) == target_col
        )
    first = first_ref[0]
    leaf_base = first_ref[1]
    stride = first_ref[2]
    slots_ref[:prim, :] = iota((prim, LANES), 0) + first
    label = owner * stride + leaf_base + row_ref[...]
    slots_ref[prim:, :] = jnp.broadcast_to(label, (LANES, n)).T
    wrow_ref[...] = (wt_ref[...].astype(F32).T * 0.5).astype(BF16)
    bucket = bucket_ref[...]
    value = jnp.zeros(bucket.shape, F32)
    for b in range(prop_ref.shape[0]):
        value = jnp.where(bucket == b, prop_ref[b], value)
    value_ref[...] = value * weight_ref[...] * 0.5


def grad_kernel(
    core_ref, comp_ref, comp_t_ref, slots_ref, wrow_ref, wt_ref, arrived_ref, label_ref, value_ref, weight_ref,
    sib_ref, own_ref,
    part_sib_ref, part_own_ref, prim_ref, back_ref,
    w_scr, wt_scr, logit_scr, coef_scr, copy_scr,
):
    prim = wt_ref.shape[1]
    slots = slots_ref.shape[0]
    dim = wt_ref.shape[0]
    arrived = arrived_ref[...].reshape(-1, dim)
    copies = nn(comp_ref[...], arrived)
    w_scr[:prim, :] = wrow_ref[...]
    w_scr[prim:, :] = (copies * 0.5).astype(BF16)
    wt_scr[:, :prim] = wt_ref[...]
    wt_scr[:, prim:] = copies.T.astype(BF16)
    prim_ref[...] = jnp.zeros(prim_ref.shape, F32)
    copy_scr[...] = jnp.zeros(copy_scr.shape, F32)
    core = core_ref[0]

    def half(q_ref, part_ref, which):
        def step(k, carry):
            q = jnp.concatenate([q_ref[2 * k], q_ref[2 * k + 1]], axis=1)
            logit_scr[...] = nn(w_scr[...], q)
            for side in range(2):
                block = 2 * (2 * k + side) + which
                at = pl.ds(pl.multiple_of(block * LANES, LANES), LANES)
                half_weight = weight_ref[:, at] * 0.5
                labels = label_ref[:, at]
                values = value_ref[:, at]
                lanes = slice(side * LANES, (side + 1) * LANES)
                for r in range(0, slots, ROW_CHUNK):
                    rows = slice(r, r + ROW_CHUNK)
                    t = jnp.tanh(logit_scr[rows, lanes])
                    slot = slots_ref[rows, :]
                    total = jnp.where(slot == labels[0:1, :], values[0:1, :], 0.0)
                    for p in range(1, labels.shape[0]):
                        total = total + jnp.where(slot == labels[p:p + 1, :], values[p:p + 1, :], 0.0)
                    hit = total > 0.0
                    scale = jnp.where(hit, total, half_weight)
                    coef_scr[rows, lanes] = (scale * (t + jnp.where(hit, -1.0, 1.0))).astype(BF16)
            coef = coef_scr[...]
            part = nn(wt_scr[...], coef)
            part_ref[2 * k] = part[:, :LANES]
            part_ref[2 * k + 1] = part[:, LANES:]
            prim_ref[...] += nt(q, coef[:prim])
            copy_scr[...] += nt(coef[prim:], q)
            return carry

        lax.fori_loop(0, q_ref.shape[0] // 2, step, 0)

    half(sib_ref, part_sib_ref, 1 - core)
    half(own_ref, part_own_ref, core)
    back = nn(comp_t_ref[...], copy_scr[...].astype(BF16))
    back_ref[...] = back.astype(BF16).reshape(back_ref.shape)


def finish_kernel(ask_ref, prim_ref, returned_ref, out_ref):
    ask = ask_ref[...].reshape(ask_ref.shape[0], LANES)
    hot = wanted_hot(ask, prim_ref.shape[1])
    returned = returned_ref[...].reshape(-1, prim_ref.shape[0])
    out_ref[...] = prim_ref[...] + tn(returned, hot)


def on_device(
    query_feats, query_weight, positive_label, positive_bucket, inv_prop, primary_w, copy_owner, copy_row
):
    sections = lax.axis_size("section")
    leaves = lax.axis_size("leaf")
    section_id = lax.axis_index("section")
    leaf_id = lax.axis_index("leaf")
    prim, dim = primary_w.shape
    n = copy_owner.shape[0]
    slots = prim + n
    chips = leaves // 2
    same_core = [[2 * y + c for y in range(chips)] for c in range(2)]
    sibling = [(i, i ^ 1) for i in range(leaves)]
    queries = query_feats.shape[0]
    shape = jax.ShapeDtypeStruct

    owner = copy_owner.reshape(1, n)
    row = copy_row.reshape(1, n)
    wt = primary_w.T
    qt = query_feats.T

    ask = call(ask_kernel, shape((sections, 1, LANES), F32), [VMEM] * 2)(owner, row)
    wanted = lax.all_to_all(ask, "section", split_axis=0, concat_axis=0, tiled=True)
    q_own = lax.all_gather(qt, "leaf", axis=0, tiled=False, axis_index_groups=same_core)
    q_sib = lax.ppermute(q_own, "leaf", sibling)
    served = call(serve_kernel, shape((sections, CAP, dim), BF16), [VMEM] * 2)(wanted, wt)
    arrived = lax.all_to_all(served, "section", split_axis=0, concat_axis=0, tiled=True)

    first = (section_id * leaves + leaf_id) * prim
    numbers = jnp.stack([first, leaf_id * prim, jnp.int32(leaves * prim)]).astype(I32)
    weight = query_weight.reshape(1, -1)
    comp, comp_t, slot_ids, wrow, value = call(
        prepare_kernel,
        (
            shape((n, sections * CAP), BF16),
            shape((sections * CAP, n), BF16),
            shape((slots, LANES), I32),
            shape((prim, dim), BF16),
            shape(positive_label.shape[::-1], F32),
        ),
        [SMEM, SMEM] + [VMEM] * 5,
    )(numbers, inv_prop, owner, row, wt, positive_bucket.T, weight)

    core = (leaf_id % 2).reshape(1).astype(I32)
    part_sib, part_own, prim_t, back = call(
        grad_kernel,
        (
            shape((chips, dim, queries), F32),
            shape((chips, dim, queries), F32),
            shape((dim, prim), F32),
            shape((sections, CAP, dim), BF16),
        ),
        [SMEM] + [VMEM] * 11,
        scratch=(
            pltpu.VMEM((slots, dim), BF16),
            pltpu.VMEM((dim, slots), BF16),
            pltpu.VMEM((slots, 2 * LANES), F32),
            pltpu.VMEM((slots, 2 * LANES), BF16),
            pltpu.VMEM((n, dim), F32),
        ),
    )(core, comp, comp_t, slot_ids, wrow, wt, arrived, positive_label.T, value, weight, q_sib, q_own)

    other = lax.ppermute(part_sib, "leaf", sibling)
    returned = lax.all_to_all(back, "section", split_axis=0, concat_axis=0, tiled=True)
    pair = (part_own + other).astype(BF16)
    pieces = lax.all_to_all(pair, "leaf", split_axis=0, concat_axis=0, axis_index_groups=same_core, tiled=True)
    query_grad = jnp.sum(pieces.astype(F32), axis=0)
    prim_grad = call(finish_kernel, shape((dim, prim), F32), [VMEM] * 3)(wanted, prim_t, returned)
    return query_grad.T, prim_grad.T


def solution(mesh):
    placed = (
        P(("section", "leaf"), None),
        P("section"),
        P("section", None),
        P("section", None),
        P(),
        P(("section", "leaf"), None),
        P(("section", "leaf")),
        P(("section", "leaf")),
    )
    return jax.shard_map(
        on_device,
        mesh=mesh,
        in_specs=placed,
        out_specs=(P(("section", "leaf"), None), P(("section", "leaf"), None)),
        check_vma=False,
    )
```

```python
import jax
import jax.numpy as jnp
from jax import lax
from jax.experimental import pallas as pl
from jax.experimental.pallas import tpu as pltpu
from jax.sharding import PartitionSpec as P

BF16 = jnp.bfloat16
F32 = jnp.float32
I32 = jnp.int32
LANES = 128
CAP = 16
ROW_CHUNK = 32
BIG = 60

VMEM = pl.BlockSpec(memory_space=pltpu.VMEM)
SMEM = pl.BlockSpec(memory_space=pltpu.SMEM)
ANY = pl.BlockSpec(memory_space=pl.ANY)

HOPS = ((4, 1, 7, 0), (3, 5, 2, 6))


def iota(shape, dim):
    return lax.broadcasted_iota(I32, shape, dim)


def ones(mask):
    return jnp.where(mask, 1.0, 0.0).astype(BF16)


def nt(a, b):
    return lax.dot_general(a, b, (((1,), (1,)), ((), ())), preferred_element_type=F32)


def nn(a, b):
    return lax.dot_general(a, b, (((1,), (0,)), ((), ())), preferred_element_type=F32)


def tn(a, b):
    return lax.dot_general(a, b, (((0,), (0,)), ((), ())), preferred_element_type=F32)


def call(kernel, out, ins, scratch=(), vmem=8, outs=None):
    return pl.pallas_call(
        kernel,
        out_shape=out,
        in_specs=ins,
        out_specs=outs or jax.tree.map(lambda _: VMEM, out),
        scratch_shapes=scratch,
        compiler_params=pltpu.CompilerParams(vmem_limit_bytes=vmem * 2**20),
    )


def hops(chips, k, way):
    return [(2 * y + c, 2 * ((y + way * HOPS[c][k]) % chips) + c) for y in range(chips) for c in range(2)]


def after(values, *earlier):
    return lax.optimization_barrier((*values, *earlier))[:len(values)]


def fetch(sems, *moves):
    copies = [pltpu.make_async_copy(src, dst, sems.at[i]) for i, (src, dst) in enumerate(moves)]
    for copy in copies:
        copy.start()
    return copies


def wait(copies):
    for copy in copies:
        copy.wait()


def ranks(owner, sections):
    n = owner.shape[1]
    hot = owner == iota((sections, n), 0)
    upper = ones(iota((n, n), 0) < iota((n, n), 1))
    before = nn(ones(hot), upper)
    return hot, jnp.sum(jnp.where(hot, before, 0.0), axis=0, keepdims=True)


def pad_kernel(qt_hbm, wt_hbm, qp_ref, wp_ref, qt_ref, wt_ref, sems):
    copies = fetch(sems, (qt_hbm, qt_ref), (wt_hbm, wt_ref))
    dim = qt_hbm.shape[0]
    for copy, src, dst in zip(copies, (qt_ref, wt_ref), (qp_ref, wp_ref)):
        copy.wait()
        dst[:dim, :] = src[...]
        dst[dim:, :] = jnp.zeros((dst.shape[0] - dim, dst.shape[1]), dst.dtype)


def ask_kernel(owner_hbm, row_hbm, ask_ref, owner_ref, row_ref, sems):
    wait(fetch(sems, (owner_hbm, owner_ref), (row_hbm, row_ref)))
    sections = ask_ref.shape[0]
    owner = owner_ref[...]
    hot, rank = ranks(owner, sections)
    rows = jnp.where(hot, row_ref[...].astype(F32) + 1.0, 0.0).astype(BF16)
    place = ones(iota((LANES, owner.shape[1]), 0).astype(F32) == rank)
    ask_ref[...] = jnp.broadcast_to(nt(rows, place)[:, None, :], ask_ref.shape)


def wanted_hot(ask, prim):
    sections = ask.shape[0]
    places = sections * CAP
    spread = ones(iota((places, sections), 0) // CAP == iota((places, sections), 1))
    every = nn(spread, ask.astype(BF16))
    mine = iota((places, LANES), 0) % CAP == iota((places, LANES), 1)
    column = jnp.sum(jnp.where(mine, every, 0.0), axis=1, keepdims=True)
    return ones(iota((places, prim), 1).astype(F32) + 1.0 == column)


def serve_kernel(ask_ref, wt_ref, served_ref):
    ask = ask_ref[:, 0, :]
    hot = wanted_hot(ask, wt_ref.shape[1])
    served_ref[...] = nt(hot, wt_ref[...]).astype(BF16).reshape(served_ref.shape)


def prepare_kernel(
    first_ref, prop_ref, owner_ref, row_ref, wt_ref, bucket_ref, weight_ref,
    comp_ref, comp_t_ref, slots_ref, wrow_ref, value_ref,
):
    sections = comp_ref.shape[1] // CAP
    owner = owner_ref[...]
    prim = wt_ref.shape[1]
    n = owner.shape[1]
    _, rank = ranks(owner, sections)
    target = owner.astype(F32) * CAP + rank
    places = sections * CAP
    comp_t_ref[...] = ones(iota((places, n), 0).astype(F32) == target)
    target_col = jnp.broadcast_to(target, (LANES, n)).T
    for block in range(places // LANES):
        comp_ref[:, block * LANES:(block + 1) * LANES] = ones(
            (iota((n, LANES), 1) + block * LANES).astype(F32) == target_col
        )
    first = first_ref[0]
    leaf_base = first_ref[1]
    stride = first_ref[2]
    slots_ref[:prim, :] = iota((prim, LANES), 0) + first
    label = owner * stride + leaf_base + row_ref[...]
    slots_ref[prim:, :] = jnp.broadcast_to(label, (LANES, n)).T
    wrow_ref[...] = (wt_ref[...].astype(F32).T * 0.5).astype(BF16)
    bucket = bucket_ref[...]
    value = jnp.zeros(bucket.shape, F32)
    for b in range(prop_ref.shape[0]):
        value = jnp.where(bucket == b, prop_ref[b], value)
    value_ref[...] = value * weight_ref[...] * 0.5


def grad_kernel(
    columns_ref, arrived_hbm, q0_hbm, q1_hbm, q2_hbm, q3_hbm, sib_hbm,
    comp_hbm, comp_t_hbm, slots_hbm, wrow_hbm, wt_hbm, label_hbm, value_hbm, weight_hbm,
    part_sib_hbm, part_own_hbm, prim_hbm, back_ref,
    arrived_ref, sib_ref, own_ref, comp_ref, comp_t_ref, slots_ref, w_scr, wt_scr, label_ref, value_ref, weight_ref,
    part_ref, prim_ref, logit_scr, coef_scr, copy_scr, in_sems, out_sems,
):
    prim = wt_hbm.shape[1]
    slots = slots_ref.shape[0]
    dim = wt_hbm.shape[0]
    copies = fetch(
        in_sems,
        (arrived_hbm, arrived_ref),
        (comp_hbm, comp_ref),
        (wrow_hbm, w_scr.at[:prim, :]),
        (wt_hbm, wt_scr.at[:, :prim]),
        (sib_hbm, sib_ref),
        (slots_hbm, slots_ref),
        (label_hbm, label_ref),
        (value_hbm, value_ref),
        (weight_hbm, weight_ref),
        (q0_hbm, own_ref.at[0:2]),
        (q1_hbm, own_ref.at[2:4]),
        (q2_hbm, own_ref.at[4:6]),
        (q3_hbm, own_ref.at[6:8]),
        (comp_t_hbm, comp_t_ref),
    )
    prim_ref[...] = jnp.zeros(prim_ref.shape, F32)
    copy_scr[...] = jnp.zeros(copy_scr.shape, F32)
    wait(copies[:2])
    fetched = nn(comp_ref[...], arrived_ref[...].reshape(-1, dim))
    w_scr[prim:, :] = (fetched * 0.5).astype(BF16)
    wt_scr[:, prim:] = fetched.T.astype(BF16)
    wait(copies[2:])

    def pair(q, k):
        logit_scr[...] = nn(w_scr[...], q)
        for side in range(2):
            at = pl.ds(pl.multiple_of(columns_ref[2 * k + side] * LANES, LANES), LANES)
            half_weight = weight_ref[:, at] * 0.5
            labels = label_ref[:, at]
            values = value_ref[:, at]
            lanes = slice(side * LANES, (side + 1) * LANES)
            for r in range(0, slots, ROW_CHUNK):
                rows = slice(r, r + ROW_CHUNK)
                t = jnp.tanh(logit_scr[rows, lanes])
                slot = slots_ref[rows, :]
                total = jnp.where(slot == labels[0:1, :], values[0:1, :], 0.0)
                for p in range(1, labels.shape[0]):
                    total = total + jnp.where(slot == labels[p:p + 1, :], values[p:p + 1, :], 0.0)
                hit = total > 0.0
                scale = jnp.where(hit, total, half_weight)
                coef_scr[rows, lanes] = (scale * (t + jnp.where(hit, -1.0, 1.0))).astype(BF16)
        coef = coef_scr[...]
        prim_ref[...] += nt(q, coef[:prim])
        copy_scr[...] += nt(coef[prim:], q)
        return nn(wt_scr[...], coef)

    chips = sib_ref.shape[0] // 2

    def step(k, carry):
        sib = k < chips
        at = 2 * jnp.where(sib, k, k - chips)

        def run(q_ref, out_hbm):
            part = pair(jnp.concatenate([q_ref[at], q_ref[at + 1]], axis=1), jnp.where(sib, k + chips, k - chips))
            part_ref[2 * k] = part[:, :LANES]
            part_ref[2 * k + 1] = part[:, LANES:]
            pltpu.make_async_copy(part_ref.at[pl.ds(2 * k, 2)], out_hbm.at[pl.ds(at, 2)], out_sems.at[k]).start()

        pl.when(sib)(lambda: run(sib_ref, part_sib_hbm))
        pl.when(jnp.logical_not(sib))(lambda: run(own_ref, part_own_hbm))
        return carry

    lax.fori_loop(0, 2 * chips, step, 0)
    last = pltpu.make_async_copy(prim_ref, prim_hbm, out_sems.at[2 * chips])
    last.start()
    back = nn(comp_t_ref[...], copy_scr[...].astype(BF16))
    back_ref[...] = back.astype(BF16).reshape(back_ref.shape)
    for k in range(2 * chips):
        out_hbm = part_sib_hbm if k < chips else part_own_hbm
        at = 2 * (k % chips)
        pltpu.make_async_copy(part_ref.at[2 * k:2 * k + 2], out_hbm.at[at:at + 2], out_sems.at[k]).wait()
    last.wait()


def finish_kernel(ask_ref, prim_ref, returned_ref, out_ref):
    ask = ask_ref[:, 0, :]
    hot = wanted_hot(ask, prim_ref.shape[1])
    returned = returned_ref[...].reshape(-1, prim_ref.shape[0])
    out_ref[...] = (prim_ref[...] + tn(returned, hot))[:out_ref.shape[0]]


def on_device(
    query_feats, query_weight, positive_label, positive_bucket, inv_prop, primary_w, copy_owner, copy_row
):
    sections = lax.axis_size("section")
    leaves = lax.axis_size("leaf")
    section_id = lax.axis_index("section")
    leaf_id = lax.axis_index("leaf")
    prim, features = primary_w.shape
    n = copy_owner.shape[0]
    slots = prim + n
    chips = leaves // 2
    sibling = [(i, i ^ 1) for i in range(leaves)]
    queries = query_feats.shape[0]
    shape = jax.ShapeDtypeStruct

    owner = copy_owner.reshape(1, n)
    row = copy_row.reshape(1, n)
    dim = 16 * pl.cdiv(features, 16)

    ask = call(
        ask_kernel,
        shape((sections, 8, LANES), F32),
        [ANY] * 2,
        scratch=(pltpu.VMEM((1, n), I32), pltpu.VMEM((1, n), I32), pltpu.SemaphoreType.DMA((2,))),
        vmem=BIG,
    )(owner, row)
    wanted = lax.all_to_all(ask, "section", split_axis=0, concat_axis=0, tiled=True)
    qp, wp = call(
        pad_kernel,
        (shape((dim, queries), BF16), shape((dim, prim), BF16)),
        [ANY] * 2,
        scratch=(
            pltpu.VMEM((features, queries), BF16),
            pltpu.VMEM((features, prim), BF16),
            pltpu.SemaphoreType.DMA((2,)),
        ),
        vmem=BIG,
    )(*after((query_feats.T, primary_w.T), ask))
    both = jnp.stack([qp, lax.ppermute(qp, "leaf", sibling)])
    own = [lax.ppermute(both, "leaf", hops(chips, k, 1)) for k in range(4)]
    served = call(serve_kernel, shape((sections, CAP, dim), BF16), [VMEM] * 2)(wanted, wp)
    own = after(own, served)
    sib = lax.ppermute(jnp.concatenate(own), "leaf", sibling)
    arrived = lax.all_to_all(served, "section", split_axis=0, concat_axis=0, tiled=True)

    first = (section_id * leaves + leaf_id) * prim
    numbers = jnp.stack([first, leaf_id * prim, jnp.int32(leaves * prim)]).astype(I32)
    weight = query_weight.reshape(1, -1)
    comp, comp_t, slot_ids, wrow, value = call(
        prepare_kernel,
        (
            shape((n, sections * CAP), BF16),
            shape((sections * CAP, n), BF16),
            shape((slots, LANES), I32),
            shape((prim, dim), BF16),
            shape(positive_label.shape[::-1], F32),
        ),
        [SMEM, SMEM] + [VMEM] * 5,
        vmem=BIG,
    )(numbers, inv_prop, owner, row, wp, positive_bucket.T, weight)

    core = leaf_id % 2
    chip = leaf_id // 2
    near = jnp.array(HOPS, I32)
    mine = (chip - near[core]) % chips
    other = (chip - near[1 - core]) % chips
    ends = jnp.stack([core, 1 - core])
    columns = jnp.concatenate(
        [(2 * mine[:, None] + ends[None, :]).reshape(-1), (2 * other[:, None] + ends[None, ::-1]).reshape(-1)]
    ).astype(I32)
    total = positive_label.shape[0]
    part_sib, part_own, prim_t, back = call(
        grad_kernel,
        (
            shape((chips, dim, queries), F32),
            shape((chips, dim, queries), F32),
            shape((dim, prim), F32),
            shape((sections, CAP, dim), BF16),
        ),
        [SMEM] + [ANY] * 14,
        scratch=(
            pltpu.VMEM(arrived.shape, BF16),
            pltpu.VMEM(sib.shape, BF16),
            pltpu.VMEM(sib.shape, BF16),
            pltpu.VMEM(comp.shape, BF16),
            pltpu.VMEM(comp_t.shape, BF16),
            pltpu.VMEM((slots, LANES), I32),
            pltpu.VMEM((slots, dim), BF16),
            pltpu.VMEM((dim, slots), BF16),
            pltpu.VMEM((positive_label.shape[1], total), I32),
            pltpu.VMEM((positive_label.shape[1], total), F32),
            pltpu.VMEM((1, total), F32),
            pltpu.VMEM((leaves, dim, queries), F32),
            pltpu.VMEM((dim, prim), F32),
            pltpu.VMEM((slots, 2 * LANES), F32),
            pltpu.VMEM((slots, 2 * LANES), BF16),
            pltpu.VMEM((n, dim), F32),
            pltpu.SemaphoreType.DMA((14,)),
            pltpu.SemaphoreType.DMA((chips + 1,)),
        ),
        vmem=BIG,
        outs=(ANY, ANY, ANY, VMEM),
    )(columns, arrived, *own, sib, comp, comp_t, slot_ids, wrow, wp, positive_label.T, value, weight)

    swapped = lax.ppermute(part_sib, "leaf", sibling)
    returned = lax.all_to_all(back, "section", split_axis=0, concat_axis=0, tiled=True)
    sums = (part_own + swapped).astype(BF16)
    pieces = [lax.ppermute(sums[2 * k:2 * k + 2], "leaf", hops(chips, k, -1)) for k in range(4)]
    prim_grad = call(finish_kernel, shape((features, prim), F32), [VMEM] * 3)(wanted, prim_t, returned)
    pieces = after(pieces, prim_grad)
    gathered = sum(piece.astype(F32) for piece in pieces)
    query_grad = gathered[0] + lax.ppermute(gathered[1], "leaf", sibling)
    return query_grad[:features].T, prim_grad.T


def solution(mesh):
    placed = (
        P(("section", "leaf"), None),
        P("section"),
        P("section", None),
        P("section", None),
        P(),
        P(("section", "leaf"), None),
        P(("section", "leaf")),
        P(("section", "leaf")),
    )
    return jax.shard_map(
        on_device,
        mesh=mesh,
        in_specs=placed,
        out_specs=(P(("section", "leaf"), None), P(("section", "leaf"), None)),
        check_vma=False,
    )
```

```python
import jax
import jax.numpy as jnp
from jax import lax
from jax.experimental import pallas as pl
from jax.experimental.pallas import tpu as pltpu
from jax.sharding import PartitionSpec as P

BF16 = jnp.bfloat16
F32 = jnp.float32
I32 = jnp.int32
LANES = 128
CAP = 16
ROW_CHUNK = 32
STEP = 8
FEW = 4
BIG = 60

VMEM = pl.BlockSpec(memory_space=pltpu.VMEM)
SMEM = pl.BlockSpec(memory_space=pltpu.SMEM)
ANY = pl.BlockSpec(memory_space=pl.ANY)

HOPS = ((0, 7, 1, 4), (6, 2, 5, 3))


def iota(shape, dim):
    return lax.broadcasted_iota(I32, shape, dim)


def ones(mask):
    return jnp.where(mask, 1.0, 0.0).astype(BF16)


def nt(a, b):
    return lax.dot_general(a, b, (((1,), (1,)), ((), ())), preferred_element_type=F32)


def nn(a, b):
    return lax.dot_general(a, b, (((1,), (0,)), ((), ())), preferred_element_type=F32)


def tn(a, b):
    return lax.dot_general(a, b, (((0,), (0,)), ((), ())), preferred_element_type=F32)


def call(kernel, out, ins, scratch=(), vmem=8, outs=None):
    return pl.pallas_call(
        kernel,
        out_shape=out,
        in_specs=ins,
        out_specs=outs or jax.tree.map(lambda _: VMEM, out),
        scratch_shapes=scratch,
        compiler_params=pltpu.CompilerParams(vmem_limit_bytes=vmem * 2**20),
    )


def hops(chips, k, way):
    return [(2 * y + c, 2 * ((y + way * HOPS[c][k]) % chips) + c) for y in range(chips) for c in range(2)]


def after(values, *earlier):
    return lax.optimization_barrier((*values, *earlier))[:len(values)]


def fetch(sems, *moves):
    copies = [pltpu.make_async_copy(src, dst, sems.at[i]) for i, (src, dst) in enumerate(moves)]
    for copy in copies:
        copy.start()
    return copies


def wait(copies):
    for copy in copies:
        copy.wait()


def ranks(owner, sections):
    n = owner.shape[1]
    hot = owner == iota((sections, n), 0)
    upper = ones(iota((n, n), 0) < iota((n, n), 1))
    before = nn(ones(hot), upper)
    return hot, jnp.sum(jnp.where(hot, before, 0.0), axis=0, keepdims=True)


def start_kernel(
    owner_hbm, row_hbm, qt_hbm, wt_hbm, ask_ref, qp_ref, wp_ref, owner_ref, row_ref, qt_ref, wt_ref, sems
):
    copies = fetch(sems, (owner_hbm, owner_ref), (row_hbm, row_ref), (qt_hbm, qt_ref), (wt_hbm, wt_ref))
    dim = qt_hbm.shape[0]
    for dst in (qp_ref, wp_ref):
        dst[dim:, :] = jnp.zeros((dst.shape[0] - dim, dst.shape[1]), dst.dtype)
    wait(copies)
    qp_ref[:dim, :] = qt_ref[...]
    wp_ref[:dim, :] = wt_ref[...]
    sections = ask_ref.shape[0]
    owner = owner_ref[...]
    hot, rank = ranks(owner, sections)
    rows = jnp.where(hot, row_ref[...].astype(F32) + 1.0, 0.0).astype(BF16)
    place = ones(iota((LANES, owner.shape[1]), 0).astype(F32) == rank)
    ask_ref[...] = jnp.broadcast_to(nt(rows, place)[:, None, :], ask_ref.shape)


def wanted_hot(ask, prim):
    sections = ask.shape[0]
    places = sections * CAP
    spread = ones(iota((places, sections), 0) // CAP == iota((places, sections), 1))
    every = nn(spread, ask.astype(BF16))
    mine = iota((places, LANES), 0) % CAP == iota((places, LANES), 1)
    column = jnp.sum(jnp.where(mine, every, 0.0), axis=1, keepdims=True)
    return ones(iota((places, prim), 1).astype(F32) + 1.0 == column)


def serve_kernel(ask_ref, wt_ref, served_ref):
    ask = ask_ref[:, 0, :]
    hot = wanted_hot(ask, wt_ref.shape[1])
    served_ref[...] = nt(hot, wt_ref[...]).astype(BF16).reshape(served_ref.shape)


def prepare_kernel(
    first_ref, prop_ref, owner_ref, row_ref, wt_ref, label_ref, bucket_ref, weight_ref,
    comp_ref, comp_t_ref, slots_ref, wrow_ref, key_ref, value_ref, count_ref,
):
    sections = comp_ref.shape[1] // CAP
    owner = owner_ref[...]
    prim = wt_ref.shape[1]
    n = owner.shape[1]
    _, rank = ranks(owner, sections)
    target = owner.astype(F32) * CAP + rank
    places = sections * CAP
    comp_t_ref[...] = ones(iota((places, n), 0).astype(F32) == target)
    target_col = jnp.broadcast_to(target, (LANES, n)).T
    for block in range(places // LANES):
        comp_ref[:, block * LANES:(block + 1) * LANES] = ones(
            (iota((n, LANES), 1) + block * LANES).astype(F32) == target_col
        )
    first = first_ref[0]
    leaf_base = first_ref[1]
    stride = first_ref[2]
    slots_ref[:prim, :] = iota((prim, LANES), 0) + first
    label = owner * stride + leaf_base + row_ref[...]
    slots_ref[prim:, :] = jnp.broadcast_to(label, (LANES, n)).T
    wrow_ref[...] = (wt_ref[...].astype(F32).T * 0.5).astype(BF16)
    bucket = bucket_ref[...]
    value = jnp.zeros(bucket.shape, F32)
    for b in range(prop_ref.shape[0]):
        value = jnp.where(bucket == b, prop_ref[b], value)
    value = value * weight_ref[...] * 0.5
    positives = label_ref[...]
    shift = prim.bit_length() - 1
    leaf_mask = stride // prim - 1
    here = jnp.where((positives >> shift) & leaf_mask == leaf_base >> shift, 1, 0)
    places = positives.shape[0]
    keys = [jnp.full((1, positives.shape[1]), -1, I32)] * places
    values = [jnp.zeros((1, positives.shape[1]), F32)] * places
    count = jnp.zeros((1, positives.shape[1]), I32)
    for p in range(places):
        at = jnp.where(here[p:p + 1] == 1, count, places)
        for k in range(p + 1):
            keys[k] = jnp.where(at == k, positives[p:p + 1], keys[k])
            values[k] = jnp.where(at == k, value[p:p + 1], values[k])
        count = count + here[p:p + 1]
    for k in range(places):
        key_ref[k:k + 1, :] = keys[k]
        value_ref[k:k + 1, :] = values[k]
    for b in range(count_ref.shape[0]):
        count_ref[b] = jnp.max(count[:, b * LANES:(b + 1) * LANES].astype(F32)).astype(I32)


def grad_kernel(
    columns_ref, count_ref, arrived_hbm, q0_hbm, q1_hbm, q2_hbm, q3_hbm, sib_hbm,
    comp_hbm, comp_t_hbm, slots_hbm, wrow_hbm, wt_hbm, label_hbm, value_hbm, weight_hbm,
    part_sib_hbm, part_own_hbm, prim_hbm, back_ref,
    arrived_ref, q_ref, comp_ref, comp_t_ref, slots_ref, w_scr, wt_scr, label_ref, value_ref, weight_ref,
    part_ref, prim_ref, logit_scr, coef_scr, copy_scr, in_sems, out_sems,
):
    prim = wt_hbm.shape[1]
    slots = slots_ref.shape[0]
    dim = wt_hbm.shape[0]
    half = sib_hbm.shape[0]
    copies = fetch(
        in_sems,
        (arrived_hbm, arrived_ref),
        (comp_hbm, comp_ref),
        (wrow_hbm, w_scr.at[:prim, :]),
        (wt_hbm, wt_scr.at[:, :prim]),
        (sib_hbm, q_ref.at[:half]),
        (slots_hbm, slots_ref),
        (label_hbm, label_ref),
        (value_hbm, value_ref),
        (weight_hbm, weight_ref),
        (q0_hbm, q_ref.at[half + 0:half + 2]),
        (q1_hbm, q_ref.at[half + 2:half + 4]),
        (q2_hbm, q_ref.at[half + 4:half + 6]),
        (q3_hbm, q_ref.at[half + 6:half + 8]),
        (comp_t_hbm, comp_t_ref),
    )
    prim_ref[...] = jnp.zeros(prim_ref.shape, F32)
    copy_scr[...] = jnp.zeros(copy_scr.shape, F32)
    wait(copies[:2])
    fetched = nn(comp_ref[...], arrived_ref[...].reshape(-1, dim))
    w_scr[prim:, :] = (fetched * 0.5).astype(BF16)
    wt_scr[:, prim:] = fetched.T.astype(BF16)
    wait(copies[2:])

    def fill(side, column, depth):
        at = pl.ds(pl.multiple_of(column * LANES, LANES), LANES)
        half_weight = weight_ref[:, at] * 0.5
        labels = label_ref[:, at]
        values = value_ref[:, at]
        lanes = slice(side * LANES, (side + 1) * LANES)
        for r in range(0, slots, ROW_CHUNK):
            rows = slice(r, r + ROW_CHUNK)
            t = jnp.tanh(logit_scr[rows, lanes])
            slot = slots_ref[rows, :]
            total = jnp.where(slot == labels[0:1, :], values[0:1, :], 0.0)
            for p in range(1, depth):
                total = total + jnp.where(slot == labels[p:p + 1, :], values[p:p + 1, :], 0.0)
            hit = total > 0.0
            scale = jnp.where(hit, total, half_weight)
            coef_scr[rows, lanes] = (scale * (t + jnp.where(hit, -1.0, 1.0))).astype(BF16)

    def step(k, carry):
        first = k * STEP
        q = jnp.concatenate([q_ref[first + i] for i in range(STEP)], axis=1)
        logit_scr[...] = nn(w_scr[...], q)
        for side in range(STEP):
            column = columns_ref[first + side]
            few = count_ref[column] <= FEW
            pl.when(few)(lambda: fill(side, column, FEW))
            pl.when(jnp.logical_not(few))(lambda: fill(side, column, label_ref.shape[0]))
        coef = coef_scr[...]
        part = nn(wt_scr[...], coef)
        for i in range(STEP):
            part_ref[first + i] = part[:, i * LANES:(i + 1) * LANES]
        source = part_ref.at[pl.ds(first, STEP)]

        @pl.when(first < half)
        def _():
            pltpu.make_async_copy(source, part_sib_hbm.at[pl.ds(first, STEP)], out_sems.at[k]).start()

        @pl.when(first >= half)
        def _():
            pltpu.make_async_copy(source, part_own_hbm.at[pl.ds(first - half, STEP)], out_sems.at[k]).start()

        prim_ref[...] += nt(q, coef[:prim])
        copy_scr[...] += nt(coef[prim:], q)
        return carry

    steps = 2 * half // STEP
    lax.fori_loop(0, steps, step, 0)
    last = pltpu.make_async_copy(prim_ref, prim_hbm, out_sems.at[steps])
    last.start()
    back = nn(comp_t_ref[...], copy_scr[...].astype(BF16))
    back_ref[...] = back.astype(BF16).reshape(back_ref.shape)
    for k in range(steps):
        first = k * STEP
        out_hbm, at = (part_sib_hbm, first) if first < half else (part_own_hbm, first - half)
        pltpu.make_async_copy(
            part_ref.at[first:first + STEP], out_hbm.at[at:at + STEP], out_sems.at[k]
        ).wait()
    last.wait()


def finish_kernel(ask_ref, prim_ref, returned_ref, out_ref):
    ask = ask_ref[:, 0, :]
    hot = wanted_hot(ask, prim_ref.shape[1])
    returned = returned_ref[...].reshape(-1, prim_ref.shape[0])
    out_ref[...] = (prim_ref[...] + tn(returned, hot))[:out_ref.shape[0]]


def on_device(
    query_feats, query_weight, positive_label, positive_bucket, inv_prop, primary_w, copy_owner, copy_row
):
    sections = lax.axis_size("section")
    leaves = lax.axis_size("leaf")
    section_id = lax.axis_index("section")
    leaf_id = lax.axis_index("leaf")
    prim, features = primary_w.shape
    n = copy_owner.shape[0]
    slots = prim + n
    chips = leaves // 2
    sibling = [(i, i ^ 1) for i in range(leaves)]
    queries = query_feats.shape[0]
    shape = jax.ShapeDtypeStruct

    owner = copy_owner.reshape(1, n)
    row = copy_row.reshape(1, n)
    dim = 16 * pl.cdiv(features, 16)

    ask, qp, wp = call(
        start_kernel,
        (shape((sections, 8, LANES), F32), shape((dim, queries), BF16), shape((dim, prim), BF16)),
        [ANY] * 4,
        scratch=(
            pltpu.VMEM((1, n), I32),
            pltpu.VMEM((1, n), I32),
            pltpu.VMEM((features, queries), BF16),
            pltpu.VMEM((features, prim), BF16),
            pltpu.SemaphoreType.DMA((4,)),
        ),
        vmem=BIG,
    )(owner, row, query_feats.T, primary_w.T)
    wanted = lax.all_to_all(ask, "section", split_axis=0, concat_axis=0, tiled=True)
    both = jnp.stack([qp, lax.ppermute(qp, "leaf", sibling)])
    own = [lax.ppermute(both, "leaf", hops(chips, k, 1)) for k in range(4)]
    served = call(serve_kernel, shape((sections, CAP, dim), BF16), [VMEM] * 2)(wanted, wp)
    own = after(own, served)
    sib = lax.ppermute(jnp.concatenate(own), "leaf", sibling)
    arrived = lax.all_to_all(served, "section", split_axis=0, concat_axis=0, tiled=True)

    first = (section_id * leaves + leaf_id) * prim
    numbers = jnp.stack([first, leaf_id * prim, jnp.int32(leaves * prim)]).astype(I32)
    weight = query_weight.reshape(1, -1)
    comp, comp_t, slot_ids, wrow, key, value, count = call(
        prepare_kernel,
        (
            shape((n, sections * CAP), BF16),
            shape((sections * CAP, n), BF16),
            shape((slots, LANES), I32),
            shape((prim, dim), BF16),
            shape(positive_label.shape[::-1], I32),
            shape(positive_label.shape[::-1], F32),
            shape((leaves,), I32),
        ),
        [SMEM, SMEM] + [VMEM] * 6,
        vmem=BIG,
        outs=(VMEM,) * 6 + (SMEM,),
    )(numbers, inv_prop, owner, row, wp, positive_label.T, positive_bucket.T, weight)

    core = leaf_id % 2
    chip = leaf_id // 2
    near = jnp.array(HOPS, I32)
    mine = (chip - near[core]) % chips
    other = (chip - near[1 - core]) % chips
    ends = jnp.stack([core, 1 - core])
    columns = jnp.concatenate(
        [(2 * other[:, None] + ends[None, ::-1]).reshape(-1), (2 * mine[:, None] + ends[None, :]).reshape(-1)]
    ).astype(I32)
    total = positive_label.shape[0]
    part_sib, part_own, prim_t, back = call(
        grad_kernel,
        (
            shape((chips, dim, queries), F32),
            shape((chips, dim, queries), F32),
            shape((dim, prim), F32),
            shape((sections, CAP, dim), BF16),
        ),
        [SMEM] * 2 + [ANY] * 14,
        scratch=(
            pltpu.VMEM(arrived.shape, BF16),
            pltpu.VMEM((leaves, dim, queries), BF16),
            pltpu.VMEM(comp.shape, BF16),
            pltpu.VMEM(comp_t.shape, BF16),
            pltpu.VMEM((slots, LANES), I32),
            pltpu.VMEM((slots, dim), BF16),
            pltpu.VMEM((dim, slots), BF16),
            pltpu.VMEM((positive_label.shape[1], total), I32),
            pltpu.VMEM((positive_label.shape[1], total), F32),
            pltpu.VMEM((1, total), F32),
            pltpu.VMEM((leaves, dim, queries), F32),
            pltpu.VMEM((dim, prim), F32),
            pltpu.VMEM((slots, STEP * LANES), F32),
            pltpu.VMEM((slots, STEP * LANES), BF16),
            pltpu.VMEM((n, dim), F32),
            pltpu.SemaphoreType.DMA((14,)),
            pltpu.SemaphoreType.DMA((leaves // STEP + 1,)),
        ),
        vmem=BIG,
        outs=(ANY, ANY, ANY, VMEM),
    )(columns, count, arrived, *own, sib, comp, comp_t, slot_ids, wrow, wp, key, value, weight)

    swapped = lax.ppermute(part_sib, "leaf", sibling)
    returned = lax.all_to_all(back, "section", split_axis=0, concat_axis=0, tiled=True)
    sums = (part_own + swapped).astype(BF16)
    pieces = [lax.ppermute(sums[2 * k:2 * k + 2], "leaf", hops(chips, k, -1)) for k in range(4)]
    prim_grad = call(finish_kernel, shape((features, prim), F32), [VMEM] * 3)(wanted, prim_t, returned)
    pieces = after(pieces, prim_grad)
    gathered = sum(piece.astype(F32) for piece in pieces)
    query_grad = gathered[0] + lax.ppermute(gathered[1], "leaf", sibling)
    return query_grad[:features].T, prim_grad.T


def solution(mesh):
    placed = (
        P(("section", "leaf"), None),
        P("section"),
        P("section", None),
        P("section", None),
        P(),
        P(("section", "leaf"), None),
        P(("section", "leaf")),
        P(("section", "leaf")),
    )
    return jax.shard_map(
        on_device,
        mesh=mesh,
        in_specs=placed,
        out_specs=(P(("section", "leaf"), None), P(("section", "leaf"), None)),
        check_vma=False,
    )
```

```python
import jax
import jax.numpy as jnp
from jax import lax
from jax.experimental import pallas as pl
from jax.experimental.pallas import tpu as pltpu
from jax.sharding import PartitionSpec as P

BF16 = jnp.bfloat16
F32 = jnp.float32
I32 = jnp.int32
LANES = 128
CAP = 16
ROW_CHUNK = 32
STEP = 8
FEW = 4
BIG = 60

VMEM = pl.BlockSpec(memory_space=pltpu.VMEM)
SMEM = pl.BlockSpec(memory_space=pltpu.SMEM)
ANY = pl.BlockSpec(memory_space=pl.ANY)

HOPS = ((0, 7, 1, 4), (6, 2, 5, 3))


def iota(shape, dim):
    return lax.broadcasted_iota(I32, shape, dim)


def ones(mask):
    return jnp.where(mask, 1.0, 0.0).astype(BF16)


def nt(a, b):
    return lax.dot_general(a, b, (((1,), (1,)), ((), ())), preferred_element_type=F32)


def nn(a, b):
    return lax.dot_general(a, b, (((1,), (0,)), ((), ())), preferred_element_type=F32)


def tn(a, b):
    return lax.dot_general(a, b, (((0,), (0,)), ((), ())), preferred_element_type=F32)


def call(kernel, out, ins, scratch=(), vmem=8, outs=None):
    return pl.pallas_call(
        kernel,
        out_shape=out,
        in_specs=ins,
        out_specs=outs or jax.tree.map(lambda _: VMEM, out),
        scratch_shapes=scratch,
        compiler_params=pltpu.CompilerParams(vmem_limit_bytes=vmem * 2**20),
    )


def hops(chips, k, way):
    return [(2 * y + c, 2 * ((y + way * HOPS[c][k]) % chips) + c) for y in range(chips) for c in range(2)]


def after(values, *earlier):
    return lax.optimization_barrier((*values, *earlier))[:len(values)]


def fetch(sems, *moves):
    copies = [pltpu.make_async_copy(src, dst, sems.at[i]) for i, (src, dst) in enumerate(moves)]
    for copy in copies:
        copy.start()
    return copies


def wait(copies):
    for copy in copies:
        copy.wait()


def ranks(owner, sections):
    n = owner.shape[1]
    hot = owner == iota((sections, n), 0)
    upper = ones(iota((n, n), 0) < iota((n, n), 1))
    before = nn(ones(hot), upper)
    return hot, jnp.sum(jnp.where(hot, before, 0.0), axis=0, keepdims=True)


def start_kernel(
    owner_hbm, row_hbm, qt_hbm, wt_hbm, ask_ref, qp_ref, wp_ref, owner_ref, row_ref, qt_ref, wt_ref, sems
):
    copies = fetch(sems, (owner_hbm, owner_ref), (row_hbm, row_ref), (qt_hbm, qt_ref), (wt_hbm, wt_ref))
    dim = qt_hbm.shape[0]
    for dst in (qp_ref, wp_ref):
        dst[dim:, :] = jnp.zeros((dst.shape[0] - dim, dst.shape[1]), dst.dtype)
    wait(copies)
    qp_ref[:dim, :] = qt_ref[...]
    wp_ref[:dim, :] = wt_ref[...]
    sections = ask_ref.shape[0]
    owner = owner_ref[...]
    hot, rank = ranks(owner, sections)
    rows = jnp.where(hot, row_ref[...].astype(F32) + 1.0, 0.0).astype(BF16)
    place = ones(iota((LANES, owner.shape[1]), 0).astype(F32) == rank)
    ask_ref[...] = jnp.broadcast_to(nt(rows, place)[:, None, :], ask_ref.shape)


def wanted_hot(ask, prim):
    sections = ask.shape[0]
    places = sections * CAP
    spread = ones(iota((places, sections), 0) // CAP == iota((places, sections), 1))
    every = nn(spread, ask.astype(BF16))
    mine = iota((places, LANES), 0) % CAP == iota((places, LANES), 1)
    column = jnp.sum(jnp.where(mine, every, 0.0), axis=1, keepdims=True)
    return ones(iota((places, prim), 1).astype(F32) + 1.0 == column)


def serve_kernel(ask_ref, wt_ref, served_ref):
    ask = ask_ref[:, 0, :]
    hot = wanted_hot(ask, wt_ref.shape[1])
    served_ref[...] = nt(hot, wt_ref[...]).astype(BF16).reshape(served_ref.shape)


def prepare_kernel(
    first_ref, prop_ref, owner_ref, row_ref, wt_ref, label_ref, bucket_ref, weight_ref,
    comp_ref, comp_t_ref, slots_ref, wrow_ref, key_ref, value_ref, count_ref,
):
    sections = comp_ref.shape[1] // CAP
    owner = owner_ref[...]
    prim = wt_ref.shape[1]
    n = owner.shape[1]
    _, rank = ranks(owner, sections)
    target = owner.astype(F32) * CAP + rank
    places = sections * CAP
    comp_t_ref[...] = ones(iota((places, n), 0).astype(F32) == target)
    target_col = jnp.broadcast_to(target, (LANES, n)).T
    for block in range(places // LANES):
        comp_ref[:, block * LANES:(block + 1) * LANES] = ones(
            (iota((n, LANES), 1) + block * LANES).astype(F32) == target_col
        )
    first = first_ref[0]
    leaf_base = first_ref[1]
    stride = first_ref[2]
    slots_ref[:prim, :] = iota((prim, LANES), 0) + first
    label = owner * stride + leaf_base + row_ref[...]
    slots_ref[prim:, :] = jnp.broadcast_to(label, (LANES, n)).T
    wrow_ref[...] = (wt_ref[...].astype(F32).T * 0.5).astype(BF16)
    bucket = bucket_ref[...]
    value = jnp.zeros(bucket.shape, F32)
    for b in range(prop_ref.shape[0]):
        value = jnp.where(bucket == b, prop_ref[b], value)
    value = value * weight_ref[...] * 0.5
    positives = label_ref[...]
    shift = prim.bit_length() - 1
    leaf_mask = stride // prim - 1
    here = jnp.where((positives >> shift) & leaf_mask == leaf_base >> shift, 1, 0)
    places = positives.shape[0]
    keys = [jnp.full((1, positives.shape[1]), -1, I32)] * places
    values = [jnp.zeros((1, positives.shape[1]), F32)] * places
    count = jnp.zeros((1, positives.shape[1]), I32)
    for p in range(places):
        at = jnp.where(here[p:p + 1] == 1, count, places)
        for k in range(p + 1):
            keys[k] = jnp.where(at == k, positives[p:p + 1], keys[k])
            values[k] = jnp.where(at == k, value[p:p + 1], values[k])
        count = count + here[p:p + 1]
    for k in range(places):
        key_ref[k:k + 1, :] = keys[k]
        value_ref[k:k + 1, :] = values[k]
    for b in range(count_ref.shape[0]):
        count_ref[b] = jnp.max(count[:, b * LANES:(b + 1) * LANES].astype(F32)).astype(I32)


def grad_kernel(
    columns_ref, count_ref, arrived_hbm, q0_hbm, q1_hbm, q2_hbm, q3_hbm, sib0_hbm, sib1_hbm,
    comp_hbm, comp_t_hbm, slots_hbm, wrow_hbm, wt_hbm, label_hbm, value_hbm, weight_hbm,
    part_sib_hbm, part_own_hbm, prim_hbm, back_ref,
    arrived_ref, q_ref, comp_ref, comp_t_ref, slots_ref, w_scr, wt_scr, label_ref, value_ref, weight_ref,
    part_ref, prim_ref, logit_scr, coef_scr, copy_scr, in_sems, out_sems,
):
    prim = wt_hbm.shape[1]
    slots = slots_ref.shape[0]
    dim = wt_hbm.shape[0]
    half = 2 * sib0_hbm.shape[0]
    copies = fetch(
        in_sems,
        (arrived_hbm, arrived_ref),
        (comp_hbm, comp_ref),
        (wrow_hbm, w_scr.at[:prim, :]),
        (wt_hbm, wt_scr.at[:, :prim]),
        (sib0_hbm, q_ref.at[:half // 2]),
        (sib1_hbm, q_ref.at[half // 2:half]),
        (slots_hbm, slots_ref),
        (label_hbm, label_ref),
        (value_hbm, value_ref),
        (weight_hbm, weight_ref),
        (q0_hbm, q_ref.at[half + 0:half + 2]),
        (q1_hbm, q_ref.at[half + 2:half + 4]),
        (q2_hbm, q_ref.at[half + 4:half + 6]),
        (q3_hbm, q_ref.at[half + 6:half + 8]),
        (comp_t_hbm, comp_t_ref),
    )
    prim_ref[...] = jnp.zeros(prim_ref.shape, F32)
    copy_scr[...] = jnp.zeros(copy_scr.shape, F32)
    wait(copies[:2])
    fetched = nn(comp_ref[...], arrived_ref[...].reshape(-1, dim))
    w_scr[prim:, :] = (fetched * 0.5).astype(BF16)
    wt_scr[:, prim:] = fetched.T.astype(BF16)
    wait(copies[2:])

    def fill(side, column, depth):
        at = pl.ds(pl.multiple_of(column * LANES, LANES), LANES)
        half_weight = weight_ref[:, at] * 0.5
        labels = label_ref[:, at]
        values = value_ref[:, at]
        lanes = slice(side * LANES, (side + 1) * LANES)
        for r in range(0, slots, ROW_CHUNK):
            rows = slice(r, r + ROW_CHUNK)
            t = jnp.tanh(logit_scr[rows, lanes])
            slot = slots_ref[rows, :]
            total = jnp.where(slot == labels[0:1, :], values[0:1, :], 0.0)
            for p in range(1, depth):
                total = total + jnp.where(slot == labels[p:p + 1, :], values[p:p + 1, :], 0.0)
            hit = total > 0.0
            scale = jnp.where(hit, total, half_weight)
            coef_scr[rows, lanes] = (scale * (t + jnp.where(hit, -1.0, 1.0))).astype(BF16)

    def step(k, carry):
        first = k * STEP
        q = jnp.concatenate([q_ref[first + i] for i in range(STEP)], axis=1)
        logit_scr[...] = nn(w_scr[...], q)
        for side in range(STEP):
            column = columns_ref[first + side]
            few = count_ref[column] <= FEW
            pl.when(few)(lambda: fill(side, column, FEW))
            pl.when(jnp.logical_not(few))(lambda: fill(side, column, label_ref.shape[0]))
        coef = coef_scr[...]
        part = nn(wt_scr[...], coef)
        for i in range(STEP):
            part_ref[first + i] = part[:, i * LANES:(i + 1) * LANES]
        source = part_ref.at[pl.ds(first, STEP)]

        @pl.when(first < half)
        def _():
            pltpu.make_async_copy(source, part_sib_hbm.at[pl.ds(first, STEP)], out_sems.at[k]).start()

        @pl.when(first >= half)
        def _():
            pltpu.make_async_copy(source, part_own_hbm.at[pl.ds(first - half, STEP)], out_sems.at[k]).start()

        prim_ref[...] += nt(q, coef[:prim])
        copy_scr[...] += nt(coef[prim:], q)
        return carry

    steps = 2 * half // STEP
    lax.fori_loop(0, steps, step, 0)
    last = pltpu.make_async_copy(prim_ref, prim_hbm, out_sems.at[steps])
    last.start()
    back = nn(comp_t_ref[...], copy_scr[...].astype(BF16))
    back_ref[...] = back.astype(BF16).reshape(back_ref.shape)
    for k in range(steps):
        first = k * STEP
        out_hbm, at = (part_sib_hbm, first) if first < half else (part_own_hbm, first - half)
        pltpu.make_async_copy(
            part_ref.at[first:first + STEP], out_hbm.at[at:at + STEP], out_sems.at[k]
        ).wait()
    last.wait()


def finish_kernel(ask_ref, prim_ref, returned_ref, out_ref):
    ask = ask_ref[:, 0, :]
    hot = wanted_hot(ask, prim_ref.shape[1])
    returned = returned_ref[...].reshape(-1, prim_ref.shape[0])
    out_ref[...] = (prim_ref[...] + tn(returned, hot))[:out_ref.shape[0]]


def on_device(
    query_feats, query_weight, positive_label, positive_bucket, inv_prop, primary_w, copy_owner, copy_row
):
    sections = lax.axis_size("section")
    leaves = lax.axis_size("leaf")
    section_id = lax.axis_index("section")
    leaf_id = lax.axis_index("leaf")
    prim, features = primary_w.shape
    n = copy_owner.shape[0]
    slots = prim + n
    chips = leaves // 2
    sibling = [(i, i ^ 1) for i in range(leaves)]
    queries = query_feats.shape[0]
    shape = jax.ShapeDtypeStruct

    owner = copy_owner.reshape(1, n)
    row = copy_row.reshape(1, n)
    dim = 16 * pl.cdiv(features, 16)

    ask, qp, wp = call(
        start_kernel,
        (shape((sections, 8, LANES), F32), shape((dim, queries), BF16), shape((dim, prim), BF16)),
        [ANY] * 4,
        scratch=(
            pltpu.VMEM((1, n), I32),
            pltpu.VMEM((1, n), I32),
            pltpu.VMEM((features, queries), BF16),
            pltpu.VMEM((features, prim), BF16),
            pltpu.SemaphoreType.DMA((4,)),
        ),
        vmem=BIG,
    )(owner, row, query_feats.T, primary_w.T)
    wanted = lax.all_to_all(ask, "section", split_axis=0, concat_axis=0, tiled=True)
    both = jnp.stack([qp, lax.ppermute(qp, "leaf", sibling)])
    first = (section_id * leaves + leaf_id) * prim
    numbers = jnp.stack([first, leaf_id * prim, jnp.int32(leaves * prim)]).astype(I32)
    weight = query_weight.reshape(1, -1)
    comp, comp_t, slot_ids, wrow, key, value, count = call(
        prepare_kernel,
        (
            shape((n, sections * CAP), BF16),
            shape((sections * CAP, n), BF16),
            shape((slots, LANES), I32),
            shape((prim, dim), BF16),
            shape(positive_label.shape[::-1], I32),
            shape(positive_label.shape[::-1], F32),
            shape((leaves,), I32),
        ),
        [SMEM, SMEM] + [VMEM] * 6,
        vmem=BIG,
        outs=(VMEM,) * 6 + (SMEM,),
    )(numbers, inv_prop, owner, row, wp, positive_label.T, positive_bucket.T, weight)

    (wanted,) = after((wanted,), count)
    served = call(serve_kernel, shape((sections, CAP, dim), BF16), [VMEM] * 2)(wanted, wp)
    own = [lax.ppermute(both, "leaf", hops(chips, k, 1)) for k in range(4)]
    arrived = lax.all_to_all(served, "section", split_axis=0, concat_axis=0, tiled=True)
    late = after((jnp.concatenate(own[:2]),), arrived)[0]
    sibs = [lax.ppermute(late, "leaf", sibling), lax.ppermute(jnp.concatenate(own[2:]), "leaf", sibling)]

    core = leaf_id % 2
    chip = leaf_id // 2
    near = jnp.array(HOPS, I32)
    mine = (chip - near[core]) % chips
    other = (chip - near[1 - core]) % chips
    ends = jnp.stack([core, 1 - core])
    columns = jnp.concatenate(
        [(2 * other[:, None] + ends[None, ::-1]).reshape(-1), (2 * mine[:, None] + ends[None, :]).reshape(-1)]
    ).astype(I32)
    total = positive_label.shape[0]
    part_sib, part_own, prim_t, back = call(
        grad_kernel,
        (
            shape((chips, dim, queries), F32),
            shape((chips, dim, queries), F32),
            shape((dim, prim), F32),
            shape((sections, CAP, dim), BF16),
        ),
        [SMEM] * 2 + [ANY] * 15,
        scratch=(
            pltpu.VMEM(arrived.shape, BF16),
            pltpu.VMEM((leaves, dim, queries), BF16),
            pltpu.VMEM(comp.shape, BF16),
            pltpu.VMEM(comp_t.shape, BF16),
            pltpu.VMEM((slots, LANES), I32),
            pltpu.VMEM((slots, dim), BF16),
            pltpu.VMEM((dim, slots), BF16),
            pltpu.VMEM((positive_label.shape[1], total), I32),
            pltpu.VMEM((positive_label.shape[1], total), F32),
            pltpu.VMEM((1, total), F32),
            pltpu.VMEM((leaves, dim, queries), F32),
            pltpu.VMEM((dim, prim), F32),
            pltpu.VMEM((slots, STEP * LANES), F32),
            pltpu.VMEM((slots, STEP * LANES), BF16),
            pltpu.VMEM((n, dim), F32),
            pltpu.SemaphoreType.DMA((15,)),
            pltpu.SemaphoreType.DMA((leaves // STEP + 1,)),
        ),
        vmem=BIG,
        outs=(ANY, ANY, ANY, VMEM),
    )(columns, count, arrived, *own, *sibs, comp, comp_t, slot_ids, wrow, wp, key, value, weight)

    swapped = lax.ppermute(part_sib, "leaf", sibling)
    returned = lax.all_to_all(back, "section", split_axis=0, concat_axis=0, tiled=True)
    sums = (part_own + swapped).astype(BF16)
    pieces = [lax.ppermute(sums[2 * k:2 * k + 2], "leaf", hops(chips, k, -1)) for k in range(4)]
    prim_grad = call(finish_kernel, shape((features, prim), F32), [VMEM] * 3)(wanted, prim_t, returned)
    pieces = after(pieces, prim_grad)
    gathered = sum(piece.astype(F32) for piece in pieces)
    query_grad = gathered[0] + lax.ppermute(gathered[1], "leaf", sibling)
    return query_grad[:features].T, prim_grad.T


def solution(mesh):
    placed = (
        P(("section", "leaf"), None),
        P("section"),
        P("section", None),
        P("section", None),
        P(),
        P(("section", "leaf"), None),
        P(("section", "leaf")),
        P(("section", "leaf")),
    )
    return jax.shard_map(
        on_device,
        mesh=mesh,
        in_specs=placed,
        out_specs=(P(("section", "leaf"), None), P(("section", "leaf"), None)),
        check_vma=False,
    )
```
